32 devices in a mesh: off: 4 (over y, x), img: 8 (over z, core).
Axes of the slice: x: 2, y: 2, z: 4, core: 2. Of those that a mesh axis runs over, the one named last changes fastest.
Arguments:
- traces: bfloat16 [1024, 3072], P(('off', 'img')), may hold values from -6 to 6
- offset_bins: int32 [1024], P(('off', 'img')), may hold values from 0 to 3, as said below
- class_slots: int32 [1024], P(('off', 'img')), may hold values from 0 to 7, as said below
- weights: bfloat16 [4, 4096, 256], P('off', 'img'), may hold values from -0.375 to 0.375
- band_start: int32 [4, 32], P('off', 'img'), may hold values from 0 to 1536
- smoothing: int32 [4, 32], P('off', 'img'), may hold values from 0 to 1
Outputs:
- migrated: bfloat16 [4, 4096, 1536], P('off', 'img')
The draws below stay inside these ranges and needn't reach their ends.
Inputs may be any that keep to these rules, and one draw needn't show every extreme that they name: `offset_bins`: in each aligned block of 32 traces every class is named by exactly 8 traces. Within each aligned block of 32 traces the pairs (offset_bins, class_slots) are all distinct.
All inputs are finite; a program needn't handle non-finite values.
Results may differ from the reference program's by a relative error of at most 0.005.
Values may be sent and summed in bfloat16 or wider, within the bound.
A program may use at most 128 MiB of HBM per device.

```python
import jax
import jax.numpy as jnp
from jax import lax

NS = 3072
NT = 1536
NLEV = 2
CB = 128
TR_DEV = 32
CLASSES = 4
PER_CLASS = 8
NTR = 1024
CLASS_TR = 256
NCOL = 4096
NBLK = 32
N_OFF = 4
N_IMG = 8


def trace_order(key):
    block_keys = jax.random.split(jax.random.fold_in(key, 11), NTR // TR_DEV)
    orders = jax.vmap(lambda one_key: jax.random.permutation(one_key, TR_DEV))(block_keys)
    return orders.reshape(NTR).astype(jnp.int32)


def draw_offset_bins(key, part):
    return trace_order(key) // PER_CLASS


def draw_class_slots(key, part):
    return trace_order(key) % PER_CLASS


def set_ends(array, stream_key, smallest, top_value):
    extent = array.shape
    index_at = [jax.random.randint(jax.random.fold_in(stream_key, axis), (), 0, extent[axis]) for axis in range(len(extent))]
    array = array.at[tuple(index_at)].set(smallest)
    longest = extent.index(max(extent))
    index_at[longest] = (index_at[longest] + 1) % extent[longest]
    return array.at[tuple(index_at)].set(top_value)


def block_scale(key, dims, cuts, least, high):
    factor_of = 1.0
    for axis_at, shards_of in cuts:
        steps = jax.random.uniform(jax.random.fold_in(jax.random.fold_in(key, 6), axis_at), (shards_of,), jnp.float32, least / len(cuts), high / len(cuts))
        factor_of = factor_of * jnp.repeat(jnp.exp(steps), dims[axis_at] // shards_of).reshape((-1,) + (1,) * (len(dims) - 1 - axis_at))
    return factor_of


def centred(rng, extent, scale, reach, cuts=(), kind=jnp.bfloat16):
    drawn = jax.random.normal(rng, extent, jnp.float32) * scale
    if len(cuts) > 0:
        drawn = block_scale(rng, extent, cuts, -0.22, 0.18) * drawn
    return jnp.clip(drawn, min=-reach, max=reach).astype(kind)


def setup_inputs(seed: int = 0) -> dict:
    keys = jax.random.split(jax.random.key(seed), 7)
    return {
        "traces": centred(keys[0], (NTR, NS), 1.0, 6.0, ((0, 32),)),
        "offset_bins": draw_offset_bins(jax.random.fold_in(keys[6], 71), 0),
        "class_slots": draw_class_slots(jax.random.fold_in(keys[6], 71), 0),
        "weights": centred(keys[3], (CLASSES, NCOL, CLASS_TR), CLASS_TR ** -0.5, 0.375, ((0, 4), (1, 8))),
        "band_start": set_ends(jax.random.randint(keys[4], (CLASSES, NBLK), 0, NS - NT + 1), jax.random.fold_in(keys[4], 1), 0, NS - NT).astype(jnp.int32),
        "smoothing": set_ends(jax.random.randint(keys[5], (CLASSES, NBLK), 0, NLEV), jax.random.fold_in(keys[5], 1), 0, NLEV - 1).astype(jnp.int32),
    }


def filtered_levels(samples):
    values = samples.astype(jnp.float32)
    edges = [(0, 0)] * (values.ndim - 1)
    padded = jnp.pad(values, edges + [(1, 1)])
    boosted = values - 0.5 * (padded[..., :-2] + padded[..., 2:])
    widened = jnp.pad(boosted, edges + [(2, 2)])
    smoothed = (3.0 * boosted + 2.0 * (widened[..., 1:-3] + widened[..., 3:-1]) + widened[..., :-4] + widened[..., 4:]) / 9.0
    return jnp.stack([boosted, smoothed]).astype(jnp.bfloat16)


def reference(traces, offset_bins, class_slots, weights, band_start, smoothing):
    levels = filtered_levels(traces)
    rows_all = jnp.arange(NTR, dtype=jnp.int32)
    block_index = rows_all // TR_DEV
    source_off = block_index // N_IMG
    source_img = block_index % N_IMG
    position = (source_img * N_OFF + source_off) * PER_CLASS + class_slots
    targets = offset_bins * CLASS_TR + position
    ordered = jnp.zeros_like(levels).at[:, targets].set(levels)

    def one_block(flat_index):
        class_index = flat_index // NBLK
        block_number = flat_index % NBLK
        weight_block = lax.dynamic_slice(weights, (class_index, block_number * CB, jnp.int32(0)), (1, CB, CLASS_TR))[0]
        segment = lax.dynamic_slice(ordered, (smoothing[class_index, block_number], class_index * CLASS_TR, band_start[class_index, block_number]), (1, CLASS_TR, NT))[0]
        return jnp.dot(weight_block, segment, preferred_element_type=jnp.float32).astype(jnp.bfloat16)

    blocks = lax.map(one_block, jnp.arange(CLASSES * NBLK, dtype=jnp.int32))
    return blocks.reshape(CLASSES, NCOL, NT)
```

```python
import functools

import jax
import jax.numpy as jnp
from jax import lax
from jax.experimental import pallas as pl
from jax.experimental.pallas import tpu as pltpu
from jax.sharding import PartitionSpec as P

NT = 1536
CB = 128
MESH = pl.DeviceIdType.MESH


def gather_kernel(n_off, n_img, traces_ref, bins_ref, slots_ref, buf, send, xy_sem, up_sem, down_sem, sib_sem, recv_sem):
    o = lax.axis_index("off")
    i = lax.axis_index("img")
    rows = traces_ref.shape[0]
    per = rows // n_off
    lines = n_img // 2
    z = i // 2
    core = i % 2
    sibling = z * 2 + 1 - core
    has_up = z < lines - 1
    has_down = z > 0

    barrier = pltpu.get_barrier_semaphore()
    for step in range(1, n_off):
        pl.semaphore_signal(barrier, inc=1, device_id=((o + step) % n_off, i), device_id_type=MESH)
    pl.semaphore_signal(barrier, inc=1, device_id=(o, sibling), device_id_type=MESH)

    @pl.when(has_up)
    def _():
        pl.semaphore_signal(barrier, inc=1, device_id=(o, i + 2), device_id_type=MESH)

    @pl.when(has_down)
    def _():
        pl.semaphore_signal(barrier, inc=1, device_id=(o, i - 2), device_id_type=MESH)

    targets = bins_ref[...] * per + slots_ref[...]
    onehot = jnp.where(lax.broadcasted_iota(jnp.int32, (rows, rows), 0) == targets, 1.0, 0.0).astype(jnp.bfloat16)
    ordered = jnp.dot(onehot, traces_ref[...], preferred_element_type=jnp.float32)
    for p in range(n_off):
        send[p] = ordered[p * per:(p + 1) * per].astype(jnp.bfloat16)
    buf[i, o] = send[o]

    pl.semaphore_wait(barrier, n_off + jnp.where(has_up, 1, 0) + jnp.where(has_down, 1, 0))

    def xy_copy(step):
        p = (o + step) % n_off
        return pltpu.make_async_remote_copy(
            src_ref=send.at[p], dst_ref=buf.at[i, o], send_sem=xy_sem.at[step], recv_sem=recv_sem.at[i, o],
            device_id=(p, i), device_id_type=MESH)

    def chunk_copy(j, q, sems, target):
        return pltpu.make_async_remote_copy(
            src_ref=buf.at[j, q], dst_ref=buf.at[j, q], send_sem=sems.at[j, q], recv_sem=recv_sem.at[j, q],
            device_id=(o, target), device_id_type=MESH)

    def arrived(j, q):
        pltpu.make_async_remote_copy(
            src_ref=buf.at[j, q], dst_ref=buf.at[j, q], send_sem=sib_sem.at[j, q], recv_sem=recv_sem.at[j, q],
            device_id=(o, sibling), device_id_type=MESH).wait_recv()

    for step in range(1, n_off):
        xy_copy(step).start()

    for step in range(n_off):
        q = (o - step + n_off) % n_off
        if step > 0:
            arrived(i, q)

        @pl.when(has_up)
        def _():
            chunk_copy(i, q, up_sem, i + 2).start()

        @pl.when(has_down)
        def _():
            chunk_copy(i, q, down_sem, i - 2).start()

        chunk_copy(i, q, sib_sem, sibling).start()

    for d in range(1, lines):
        below = i - 2 * d
        above = i + 2 * d

        def one_chunk(step, carry):
            q = (o - step + n_off) % n_off

            @pl.when(z >= d)
            def _():
                arrived(below, q)

                @pl.when(has_up)
                def _():
                    chunk_copy(below, q, up_sem, i + 2).start()

                chunk_copy(below, q, sib_sem, sibling).start()

            @pl.when(z + d < lines)
            def _():
                arrived(above, q)

                @pl.when(has_down)
                def _():
                    chunk_copy(above, q, down_sem, i - 2).start()

                chunk_copy(above, q, sib_sem, sibling).start()

            return carry

        lax.fori_loop(0, n_off, one_chunk, 0)

    for w in range(lines):

        def last(q, carry):
            arrived(2 * w + 1 - core, q)
            mine = 2 * w + core
            chunk_copy(mine, q, sib_sem, sibling).wait_send()

            @pl.when(jnp.logical_and(has_up, w <= z))
            def _():
                chunk_copy(mine, q, up_sem, i + 2).wait_send()

            @pl.when(jnp.logical_and(has_down, w >= z))
            def _():
                chunk_copy(mine, q, down_sem, i - 2).wait_send()

            return carry

        lax.fori_loop(0, n_off, last, 0)

    for step in range(1, n_off):
        xy_copy(step).wait_send()


def gather_rows(traces, offset_bins, class_slots):
    n_off = lax.axis_size("off")
    n_img = lax.axis_size("img")
    rows, samples = traces.shape
    per = rows // n_off
    vmem = pl.BlockSpec(memory_space=pltpu.VMEM)
    return pl.pallas_call(
        functools.partial(gather_kernel, n_off, n_img),
        out_shape=jax.ShapeDtypeStruct((n_img, n_off, per, samples), jnp.bfloat16),
        in_specs=[vmem] * 3,
        out_specs=vmem,
        scratch_shapes=[
            pltpu.VMEM((n_off, per, samples), jnp.bfloat16),
            pltpu.SemaphoreType.DMA((n_off,)),
            pltpu.SemaphoreType.DMA((n_img, n_off)),
            pltpu.SemaphoreType.DMA((n_img, n_off)),
            pltpu.SemaphoreType.DMA((n_img, n_off)),
            pltpu.SemaphoreType.DMA((n_img, n_off)),
        ],
        compiler_params=pltpu.CompilerParams(
            collective_id=0, has_side_effects=True, vmem_limit_bytes=48 * 1024 * 1024),
        name="gather_rows",
    )(traces, offset_bins.reshape(1, rows), class_slots.reshape(1, rows))


def migrate_kernel(band_ref, smooth_ref, raw_ref, weights_ref, out_ref, levels):
    rows, samples = raw_ref.shape
    block = pl.program_id(0)

    @pl.when(block == 0)
    def _():
        gap = jnp.zeros((16, 128), jnp.float32)
        width = samples + 128

        def filter_rows(group, carry):
            at = pl.ds(pl.multiple_of(group * 16, 16), 16)
            values = jnp.concatenate([raw_ref[at, :].astype(jnp.float32), gap], axis=1)
            boosted = values - 0.5 * (pltpu.roll(values, 1, 1) + pltpu.roll(values, width - 1, 1))
            boosted = boosted[:, :samples]
            wide = jnp.concatenate([boosted, gap], axis=1)
            smoothed = (
                3.0 * wide
                + 2.0 * (pltpu.roll(wide, 1, 1) + pltpu.roll(wide, width - 1, 1))
                + pltpu.roll(wide, 2, 1)
                + pltpu.roll(wide, width - 2, 1)
            ) / 9.0
            levels[0, at, :] = boosted.astype(jnp.bfloat16)
            levels[1, at, :] = smoothed[:, :samples].astype(jnp.bfloat16)
            return carry

        lax.fori_loop(0, rows // 16, filter_rows, 0)

    start = band_ref[block]
    span = NT + 128
    base = jnp.minimum(start // 128, (samples - span) // 128) * 128
    shift = start - base
    segment = levels[smooth_ref[block], :, pl.ds(pl.multiple_of(base, 128), span)]
    product = jnp.dot(weights_ref[...], segment, preferred_element_type=jnp.float32)
    turned = pltpu.roll(product, lax.rem(span - shift, span), 1)
    out_ref[...] = turned[:, :NT].astype(jnp.bfloat16)


def migrate(raw, weight_rows, band_rows, smooth_rows):
    rows, samples = raw.shape
    columns = weight_rows.shape[0]
    return pl.pallas_call(
        migrate_kernel,
        out_shape=jax.ShapeDtypeStruct((columns, NT), jnp.bfloat16),
        grid_spec=pltpu.PrefetchScalarGridSpec(
            num_scalar_prefetch=2,
            grid=(columns // CB,),
            in_specs=[
                pl.BlockSpec((rows, samples), lambda b, *_: (0, 0)),
                pl.BlockSpec((CB, rows), lambda b, *_: (b, 0)),
            ],
            out_specs=pl.BlockSpec((CB, NT), lambda b, *_: (b, 0)),
            scratch_shapes=[pltpu.VMEM((2, rows, samples), jnp.bfloat16)],
        ),
        compiler_params=pltpu.CompilerParams(vmem_limit_bytes=48 * 1024 * 1024),
        name="migrate",
    )(band_rows, smooth_rows, raw, weight_rows)


def per_device(traces, offset_bins, class_slots, weights, band_start, smoothing):
    raw = gather_rows(traces, offset_bins, class_slots)
    raw = raw.reshape(-1, traces.shape[1])
    return migrate(raw, weights[0], band_start[0], smoothing[0])[None]


def solution(mesh):
    in_specs = (
        P(("off", "img"), None),
        P(("off", "img")),
        P(("off", "img")),
        P("off", "img", None),
        P("off", "img"),
        P("off", "img"),
    )
    out_specs = P("off", "img", None)
    return jax.shard_map(
        per_device, mesh=mesh, in_specs=in_specs, out_specs=out_specs, check_vma=False
    )
```

```python
import functools

import jax
import jax.numpy as jnp
from jax import lax
from jax.experimental import pallas as pl
from jax.experimental.pallas import tpu as pltpu
from jax.sharding import PartitionSpec as P

NT = 1536
CB = 128
MESH = pl.DeviceIdType.MESH


def gather_kernel(n_off, n_img, traces_hbm, bins_hbm, slots_hbm, out, traces_ref, bins_ref, slots_ref, buf, levels, send,
                  in_sem, xy_sem, up_sem, down_sem, sib_sem, recv_sem, out_sem):
    o = lax.axis_index("off")
    i = lax.axis_index("img")
    rows = traces_ref.shape[0]
    per = rows // n_off
    lines = n_img // 2
    z = i // 2
    core = i % 2
    sibling = z * 2 + 1 - core
    has_up = z < lines - 1
    has_down = z > 0

    inputs = [
        pltpu.make_async_copy(source, held, in_sem.at[n])
        for n, (source, held) in enumerate(
            [(traces_hbm, traces_ref), (bins_hbm, bins_ref), (slots_hbm, slots_ref)])
    ]
    for copy in inputs:
        copy.start()

    barrier = pltpu.get_barrier_semaphore()
    for step in range(1, n_off):
        pl.semaphore_signal(barrier, inc=1, device_id=((o + step) % n_off, i), device_id_type=MESH)
    pl.semaphore_signal(barrier, inc=1, device_id=(o, sibling), device_id_type=MESH)

    @pl.when(has_up)
    def _():
        pl.semaphore_signal(barrier, inc=1, device_id=(o, i + 2), device_id_type=MESH)

    @pl.when(has_down)
    def _():
        pl.semaphore_signal(barrier, inc=1, device_id=(o, i - 2), device_id_type=MESH)

    for copy in inputs:
        copy.wait()
    targets = bins_ref[...] * per + slots_ref[...]
    onehot = jnp.where(lax.broadcasted_iota(jnp.int32, (rows, rows), 0) == targets, 1.0, 0.0).astype(jnp.bfloat16)
    ordered = jnp.dot(onehot, traces_ref[...], preferred_element_type=jnp.float32)
    for p in range(n_off):
        send[p] = ordered[p * per:(p + 1) * per].astype(jnp.bfloat16)
    buf[i, o] = send[o]

    pl.semaphore_wait(barrier, n_off + jnp.where(has_up, 1, 0) + jnp.where(has_down, 1, 0))

    def xy_copy(step):
        p = (o + step) % n_off
        return pltpu.make_async_remote_copy(
            src_ref=send.at[p], dst_ref=buf.at[i, o], send_sem=xy_sem.at[step], recv_sem=recv_sem.at[i, o],
            device_id=(p, i), device_id_type=MESH)

    def chunk_copy(j, q, sems, target):
        return pltpu.make_async_remote_copy(
            src_ref=buf.at[j, q], dst_ref=buf.at[j, q], send_sem=sems.at[j, q], recv_sem=recv_sem.at[j, q],
            device_id=(o, target), device_id_type=MESH)

    def arrived(j, q):
        pltpu.make_async_remote_copy(
            src_ref=buf.at[j, q], dst_ref=buf.at[j, q], send_sem=sib_sem.at[j, q], recv_sem=recv_sem.at[j, q],
            device_id=(o, sibling), device_id_type=MESH).wait_recv()

    for step in range(1, n_off):
        xy_copy(step).start()

    def out_copy(j, q):
        return pltpu.make_async_copy(levels.at[:, j, q], out.at[:, j, q], out_sem.at[j, q])

    def filter_chunk(j, q):
        samples = buf.shape[3]
        width = samples + 128
        gap = jnp.zeros((per, 128), jnp.float32)
        values = jnp.concatenate([buf[j, q].astype(jnp.float32), gap], axis=1)
        boosted = values - 0.5 * (pltpu.roll(values, 1, 1) + pltpu.roll(values, width - 1, 1))
        boosted = boosted[:, :samples]
        wide = jnp.concatenate([boosted, gap], axis=1)
        smoothed = (
            3.0 * wide
            + 2.0 * (pltpu.roll(wide, 1, 1) + pltpu.roll(wide, width - 1, 1))
            + pltpu.roll(wide, 2, 1)
            + pltpu.roll(wide, width - 2, 1)
        ) / 9.0
        levels[0, j, q] = boosted.astype(jnp.bfloat16)
        levels[1, j, q] = smoothed[:, :samples].astype(jnp.bfloat16)
        out_copy(j, q).start()

    def first_chunk(step, carry):
        q = lax.rem(o - step + n_off, n_off)

        @pl.when(step > 0)
        def _():
            arrived(i, q)

        @pl.when(has_up)
        def _():
            chunk_copy(i, q, up_sem, i + 2).start()

        @pl.when(has_down)
        def _():
            chunk_copy(i, q, down_sem, i - 2).start()

        chunk_copy(i, q, sib_sem, sibling).start()
        filter_chunk(i, q)
        return carry

    lax.fori_loop(0, n_off, first_chunk, 0)

    def one_chunk(turn, carry):
        d = lax.div(turn, n_off) + 1
        q = lax.rem(o - lax.rem(turn, n_off) + n_off, n_off)
        below = i - 2 * d
        above = i + 2 * d
        from_below = z >= d
        from_above = z + d < lines

        @pl.when(from_below)
        def _():
            arrived(below, q)

            @pl.when(has_up)
            def _():
                chunk_copy(below, q, up_sem, i + 2).start()

            chunk_copy(below, q, sib_sem, sibling).start()

        @pl.when(from_above)
        def _():
            arrived(above, q)

            @pl.when(has_down)
            def _():
                chunk_copy(above, q, down_sem, i - 2).start()

            chunk_copy(above, q, sib_sem, sibling).start()

        @pl.when(from_below)
        def _():
            filter_chunk(below, q)

        @pl.when(from_above)
        def _():
            filter_chunk(above, q)

        near = d - 1

        @pl.when(z >= near)
        def _():
            arrived(sibling - 2 * near, q)
            filter_chunk(sibling - 2 * near, q)

        @pl.when(jnp.logical_and(near > 0, z + near < lines))
        def _():
            arrived(sibling + 2 * near, q)
            filter_chunk(sibling + 2 * near, q)

        return carry

    lax.fori_loop(0, lines * n_off, one_chunk, 0)

    for w in range(lines):

        def last(q, carry):
            mine = 2 * w + core
            out_copy(2 * w, q).wait()
            out_copy(2 * w + 1, q).wait()
            chunk_copy(mine, q, sib_sem, sibling).wait_send()

            @pl.when(jnp.logical_and(has_up, w <= z))
            def _():
                chunk_copy(mine, q, up_sem, i + 2).wait_send()

            @pl.when(jnp.logical_and(has_down, w >= z))
            def _():
                chunk_copy(mine, q, down_sem, i - 2).wait_send()

            return carry

        lax.fori_loop(0, n_off, last, 0)

    for step in range(1, n_off):
        xy_copy(step).wait_send()


def gather_levels(traces, offset_bins, class_slots):
    n_off = lax.axis_size("off")
    n_img = lax.axis_size("img")
    rows, samples = traces.shape
    per = rows // n_off
    hbm = pl.BlockSpec(memory_space=pl.ANY)
    return pl.pallas_call(
        functools.partial(gather_kernel, n_off, n_img),
        out_shape=jax.ShapeDtypeStruct((2, n_img, n_off, per, samples), jnp.bfloat16),
        in_specs=[hbm] * 3,
        out_specs=hbm,
        scratch_shapes=[
            pltpu.VMEM((rows, samples), jnp.bfloat16),
            pltpu.VMEM((1, rows), jnp.int32),
            pltpu.VMEM((1, rows), jnp.int32),
            pltpu.VMEM((n_img, n_off, per, samples), jnp.bfloat16),
            pltpu.VMEM((2, n_img, n_off, per, samples), jnp.bfloat16),
            pltpu.VMEM((n_off, per, samples), jnp.bfloat16),
            pltpu.SemaphoreType.DMA((3,)),
            pltpu.SemaphoreType.DMA((n_off,)),
            pltpu.SemaphoreType.DMA((n_img, n_off)),
            pltpu.SemaphoreType.DMA((n_img, n_off)),
            pltpu.SemaphoreType.DMA((n_img, n_off)),
            pltpu.SemaphoreType.DMA((n_img, n_off)),
            pltpu.SemaphoreType.DMA((n_img, n_off)),
        ],
        compiler_params=pltpu.CompilerParams(
            collective_id=0, has_side_effects=True, vmem_limit_bytes=56 * 1024 * 1024),
        name="gather_levels",
    )(traces, offset_bins.reshape(1, rows), class_slots.reshape(1, rows))


def migrate_kernel(band_ref, smooth_ref, levels, weights_ref, out_ref, segments, sems):
    samples = levels.shape[2]
    span = segments.shape[2]
    blocks = segments.shape[0]
    block = pl.program_id(0)

    def base_of(b):
        return jnp.minimum(lax.div(band_ref[b], 128), (samples - span) // 128) * 128

    def segment_copy(b):
        band = pl.ds(pl.multiple_of(base_of(b), 128), span)
        return pltpu.make_async_copy(levels.at[smooth_ref[b], :, band], segments.at[b], sems.at[b])

    @pl.when(block == 0)
    def _():
        for b in range(blocks):
            segment_copy(b).start()

    segment_copy(block).wait()
    shift = band_ref[block] - base_of(block)
    product = jnp.dot(weights_ref[...], segments[block], preferred_element_type=jnp.float32)
    turned = pltpu.roll(product, lax.rem(span - shift, span), 1)
    out_ref[...] = turned[:, :NT].astype(jnp.bfloat16)


def migrate(levels, weight_rows, band_rows, smooth_rows):
    rows = levels.shape[1]
    columns = weight_rows.shape[0]
    blocks = columns // CB
    return pl.pallas_call(
        migrate_kernel,
        out_shape=jax.ShapeDtypeStruct((columns, NT), jnp.bfloat16),
        grid_spec=pltpu.PrefetchScalarGridSpec(
            num_scalar_prefetch=2,
            grid=(blocks,),
            in_specs=[
                pl.BlockSpec(memory_space=pl.ANY),
                pl.BlockSpec((CB, rows), lambda b, *_: (b, 0)),
            ],
            out_specs=pl.BlockSpec((CB, NT), lambda b, *_: (b, 0)),
            scratch_shapes=[
                pltpu.VMEM((blocks, rows, NT + 128), jnp.bfloat16),
                pltpu.SemaphoreType.DMA((blocks,)),
            ],
        ),
        compiler_params=pltpu.CompilerParams(vmem_limit_bytes=48 * 1024 * 1024),
        name="migrate",
    )(band_rows, smooth_rows, levels, weight_rows)


def per_device(traces, offset_bins, class_slots, weights, band_start, smoothing):
    levels = gather_levels(traces, offset_bins, class_slots)
    levels = levels.reshape(2, -1, traces.shape[1])
    return migrate(levels, weights[0], band_start[0], smoothing[0])[None]


def solution(mesh):
    in_specs = (
        P(("off", "img"), None),
        P(("off", "img")),
        P(("off", "img")),
        P("off", "img", None),
        P("off", "img"),
        P("off", "img"),
    )
    out_specs = P("off", "img", None)
    return jax.shard_map(
        per_device, mesh=mesh, in_specs=in_specs, out_specs=out_specs, check_vma=False
    )
```

```python
import functools

import jax
import jax.numpy as jnp
from jax import lax
from jax.experimental import pallas as pl
from jax.experimental.pallas import tpu as pltpu
from jax.sharding import PartitionSpec as P

NT = 1536
CB = 128
MESH = pl.DeviceIdType.MESH


def gather_kernel(n_off, n_img, traces_hbm, bins_hbm, slots_hbm, out, traces_ref, bins_ref, slots_ref, buf, levels, send,
                  in_sem, xy_sem, up_sem, down_sem, sib_sem, recv_sem, out_sem):
    o = lax.axis_index("off")
    i = lax.axis_index("img")
    rows = traces_ref.shape[0]
    per = rows // n_off
    lines = n_img // 2
    z = i // 2
    core = i % 2
    sibling = z * 2 + 1 - core
    has_up = z < lines - 1
    has_down = z > 0

    inputs = [
        pltpu.make_async_copy(source, held, in_sem.at[n])
        for n, (source, held) in enumerate(
            [(traces_hbm, traces_ref), (bins_hbm, bins_ref), (slots_hbm, slots_ref)])
    ]
    for copy in inputs:
        copy.start()

    barrier = pltpu.get_barrier_semaphore()
    for step in range(1, n_off):
        pl.semaphore_signal(barrier, inc=1, device_id=((o + step) % n_off, i), device_id_type=MESH)
    pl.semaphore_signal(barrier, inc=1, device_id=(o, sibling), device_id_type=MESH)

    @pl.when(has_up)
    def _():
        pl.semaphore_signal(barrier, inc=1, device_id=(o, i + 2), device_id_type=MESH)

    @pl.when(has_down)
    def _():
        pl.semaphore_signal(barrier, inc=1, device_id=(o, i - 2), device_id_type=MESH)

    for copy in inputs:
        copy.wait()
    targets = bins_ref[...] * per + slots_ref[...]
    onehot = jnp.where(lax.broadcasted_iota(jnp.int32, (rows, rows), 0) == targets, 1.0, 0.0).astype(jnp.bfloat16)
    ordered = jnp.dot(onehot, traces_ref[...], preferred_element_type=jnp.float32)
    for p in range(n_off):
        send[p] = ordered[p * per:(p + 1) * per].astype(jnp.bfloat16)
    buf[i, o] = send[o]

    pl.semaphore_wait(barrier, n_off + jnp.where(has_up, 1, 0) + jnp.where(has_down, 1, 0))

    def partner(step):
        bit, total = 1, 0
        while bit < n_off:
            total = total + bit * lax.rem(lax.rem(lax.div(o, bit), 2) + lax.rem(lax.div(step, bit), 2), 2)
            bit *= 2
        return total

    def xy_copy(step):
        p = partner(jnp.int32(step))
        return pltpu.make_async_remote_copy(
            src_ref=send.at[p], dst_ref=buf.at[i, o], send_sem=xy_sem.at[step], recv_sem=recv_sem.at[i, o],
            device_id=(p, i), device_id_type=MESH)

    def chunk_copy(j, q, sems, target):
        return pltpu.make_async_remote_copy(
            src_ref=buf.at[j, q], dst_ref=buf.at[j, q], send_sem=sems.at[j, q], recv_sem=recv_sem.at[j, q],
            device_id=(o, target), device_id_type=MESH)

    def arrived(j, q):
        pltpu.make_async_remote_copy(
            src_ref=buf.at[j, q], dst_ref=buf.at[j, q], send_sem=sib_sem.at[j, q], recv_sem=recv_sem.at[j, q],
            device_id=(o, sibling), device_id_type=MESH).wait_recv()

    for step in range(1, n_off):
        xy_copy(step).start()

    def out_copy(j, q):
        return pltpu.make_async_copy(levels.at[:, j, q], out.at[:, j, q], out_sem.at[j, q])

    def filter_chunk(j, q):
        samples = buf.shape[3]
        width = samples + 128
        gap = jnp.zeros((per, 128), jnp.float32)
        values = jnp.concatenate([buf[j, q].astype(jnp.float32), gap], axis=1)
        boosted = values - 0.5 * (pltpu.roll(values, 1, 1) + pltpu.roll(values, width - 1, 1))
        boosted = boosted[:, :samples]
        wide = jnp.concatenate([boosted, gap], axis=1)
        smoothed = (
            3.0 * wide
            + 2.0 * (pltpu.roll(wide, 1, 1) + pltpu.roll(wide, width - 1, 1))
            + pltpu.roll(wide, 2, 1)
            + pltpu.roll(wide, width - 2, 1)
        ) / 9.0
        levels[0, j, q] = boosted.astype(jnp.bfloat16)
        levels[1, j, q] = smoothed[:, :samples].astype(jnp.bfloat16)
        out_copy(j, q).start()

    def first_chunk(step, carry):
        q = partner(step)

        @pl.when(step > 0)
        def _():
            arrived(i, q)

        @pl.when(has_up)
        def _():
            chunk_copy(i, q, up_sem, i + 2).start()

        @pl.when(has_down)
        def _():
            chunk_copy(i, q, down_sem, i - 2).start()

        chunk_copy(i, q, sib_sem, sibling).start()
        filter_chunk(i, q)
        return carry

    lax.fori_loop(0, n_off, first_chunk, 0)

    def one_chunk(turn, carry):
        d = lax.div(turn, n_off) + 1
        q = partner(lax.rem(turn, n_off))
        below = i - 2 * d
        above = i + 2 * d
        from_below = z >= d
        from_above = z + d < lines

        @pl.when(from_below)
        def _():
            arrived(below, q)

            @pl.when(has_up)
            def _():
                chunk_copy(below, q, up_sem, i + 2).start()

            chunk_copy(below, q, sib_sem, sibling).start()

        @pl.when(from_above)
        def _():
            arrived(above, q)

            @pl.when(has_down)
            def _():
                chunk_copy(above, q, down_sem, i - 2).start()

            chunk_copy(above, q, sib_sem, sibling).start()

        @pl.when(from_below)
        def _():
            filter_chunk(below, q)

        @pl.when(from_above)
        def _():
            filter_chunk(above, q)

        near = d - 1

        @pl.when(z >= near)
        def _():
            arrived(sibling - 2 * near, q)
            filter_chunk(sibling - 2 * near, q)

        @pl.when(jnp.logical_and(near > 0, z + near < lines))
        def _():
            arrived(sibling + 2 * near, q)
            filter_chunk(sibling + 2 * near, q)

        return carry

    lax.fori_loop(0, lines * n_off, one_chunk, 0)

    for w in range(lines):

        def last(q, carry):
            mine = 2 * w + core
            out_copy(2 * w, q).wait()
            out_copy(2 * w + 1, q).wait()
            chunk_copy(mine, q, sib_sem, sibling).wait_send()

            @pl.when(jnp.logical_and(has_up, w <= z))
            def _():
                chunk_copy(mine, q, up_sem, i + 2).wait_send()

            @pl.when(jnp.logical_and(has_down, w >= z))
            def _():
                chunk_copy(mine, q, down_sem, i - 2).wait_send()

            return carry

        lax.fori_loop(0, n_off, last, 0)

    for step in range(1, n_off):
        xy_copy(step).wait_send()


def gather_levels(traces, offset_bins, class_slots):
    n_off = lax.axis_size("off")
    n_img = lax.axis_size("img")
    rows, samples = traces.shape
    per = rows // n_off
    hbm = pl.BlockSpec(memory_space=pl.ANY)
    return pl.pallas_call(
        functools.partial(gather_kernel, n_off, n_img),
        out_shape=jax.ShapeDtypeStruct((2, n_img, n_off, per, samples), jnp.bfloat16),
        in_specs=[hbm] * 3,
        out_specs=hbm,
        scratch_shapes=[
            pltpu.VMEM((rows, samples), jnp.bfloat16),
            pltpu.VMEM((1, rows), jnp.int32),
            pltpu.VMEM((1, rows), jnp.int32),
            pltpu.VMEM((n_img, n_off, per, samples), jnp.bfloat16),
            pltpu.VMEM((2, n_img, n_off, per, samples), jnp.bfloat16),
            pltpu.VMEM((n_off, per, samples), jnp.bfloat16),
            pltpu.SemaphoreType.DMA((3,)),
            pltpu.SemaphoreType.DMA((n_off,)),
            pltpu.SemaphoreType.DMA((n_img, n_off)),
            pltpu.SemaphoreType.DMA((n_img, n_off)),
            pltpu.SemaphoreType.DMA((n_img, n_off)),
            pltpu.SemaphoreType.DMA((n_img, n_off)),
            pltpu.SemaphoreType.DMA((n_img, n_off)),
        ],
        compiler_params=pltpu.CompilerParams(
            collective_id=0, has_side_effects=True, vmem_limit_bytes=56 * 1024 * 1024),
        name="gather_levels",
    )(traces, offset_bins.reshape(1, rows), class_slots.reshape(1, rows))


def migrate_kernel(band_ref, smooth_ref, levels, weights_ref, out_ref, segments, sems):
    samples = levels.shape[2]
    span = segments.shape[2]
    blocks = segments.shape[0]
    block = pl.program_id(0)

    def base_of(b):
        return jnp.minimum(lax.div(band_ref[b], 128), (samples - span) // 128) * 128

    def segment_copy(b):
        band = pl.ds(pl.multiple_of(base_of(b), 128), span)
        return pltpu.make_async_copy(levels.at[smooth_ref[b], :, band], segments.at[b], sems.at[b])

    @pl.when(block == 0)
    def _():
        for b in range(blocks):
            segment_copy(b).start()

    segment_copy(block).wait()
    shift = band_ref[block] - base_of(block)
    product = jnp.dot(weights_ref[...], segments[block], preferred_element_type=jnp.float32)
    turned = pltpu.roll(product, lax.rem(span - shift, span), 1)
    out_ref[...] = turned[:, :NT].astype(jnp.bfloat16)


def migrate(levels, weight_rows, band_rows, smooth_rows):
    rows = levels.shape[1]
    columns = weight_rows.shape[0]
    blocks = columns // CB
    return pl.pallas_call(
        migrate_kernel,
        out_shape=jax.ShapeDtypeStruct((columns, NT), jnp.bfloat16),
        grid_spec=pltpu.PrefetchScalarGridSpec(
            num_scalar_prefetch=2,
            grid=(blocks,),
            in_specs=[
                pl.BlockSpec(memory_space=pltpu.HBM),
                pl.BlockSpec((CB, rows), lambda b, *_: (b, 0)),
            ],
            out_specs=pl.BlockSpec((CB, NT), lambda b, *_: (b, 0)),
            scratch_shapes=[
                pltpu.VMEM((blocks, rows, NT + 128), jnp.bfloat16),
                pltpu.SemaphoreType.DMA((blocks,)),
            ],
        ),
        compiler_params=pltpu.CompilerParams(vmem_limit_bytes=48 * 1024 * 1024),
        name="migrate",
    )(band_rows, smooth_rows, levels, weight_rows)


def per_device(traces, offset_bins, class_slots, weights, band_start, smoothing):
    levels = gather_levels(traces, offset_bins, class_slots)
    levels = levels.reshape(2, -1, traces.shape[1])
    return migrate(levels, weights[0], band_start[0], smoothing[0])[None]


def solution(mesh):
    in_specs = (
        P(("off", "img"), None),
        P(("off", "img")),
        P(("off", "img")),
        P("off", "img", None),
        P("off", "img"),
        P("off", "img"),
    )
    out_specs = P("off", "img", None)
    return jax.shard_map(
        per_device, mesh=mesh, in_specs=in_specs, out_specs=out_specs, check_vma=False
    )
```

```python
import functools

import jax
import jax.numpy as jnp
from jax import lax
from jax.experimental import pallas as pl
from jax.experimental.pallas import tpu as pltpu
from jax.sharding import PartitionSpec as P

NT = 1536
CB = 128
MESH = pl.DeviceIdType.MESH


def gather_kernel(n_off, n_img, traces_hbm, bins_hbm, slots_hbm, out, traces_ref, bins_ref, slots_ref, buf, levels, send,
                  in_sem, xy_sem, up_sem, down_sem, sib_sem, recv_sem, out_sem):
    o = lax.axis_index("off")
    i = lax.axis_index("img")
    rows = traces_ref.shape[0]
    per = rows // n_off
    lines = n_img // 2
    z = i // 2
    core = i % 2
    sibling = z * 2 + 1 - core
    has_up = z < lines - 1
    has_down = z > 0

    inputs = [
        pltpu.make_async_copy(source, held, in_sem.at[n])
        for n, (source, held) in enumerate(
            [(traces_hbm, traces_ref), (bins_hbm, bins_ref), (slots_hbm, slots_ref)])
    ]
    for copy in inputs:
        copy.start()

    barrier = pltpu.get_barrier_semaphore()
    for step in range(1, n_off):
        pl.semaphore_signal(barrier, inc=1, device_id=((o + step) % n_off, i), device_id_type=MESH)
    pl.semaphore_signal(barrier, inc=1, device_id=(o, sibling), device_id_type=MESH)

    @pl.when(has_up)
    def _():
        pl.semaphore_signal(barrier, inc=1, device_id=(o, i + 2), device_id_type=MESH)

    @pl.when(has_down)
    def _():
        pl.semaphore_signal(barrier, inc=1, device_id=(o, i - 2), device_id_type=MESH)

    for copy in inputs:
        copy.wait()
    targets = bins_ref[...] * per + slots_ref[...]
    onehot = jnp.where(lax.broadcasted_iota(jnp.int32, (rows, rows), 0) == targets, 1.0, 0.0).astype(jnp.bfloat16)
    ordered = jnp.dot(onehot, traces_ref[...], preferred_element_type=jnp.float32)
    for p in range(n_off):
        send[p] = ordered[p * per:(p + 1) * per].astype(jnp.bfloat16)
    buf[i, o] = send[o]

    pl.semaphore_wait(barrier, n_off + jnp.where(has_up, 1, 0) + jnp.where(has_down, 1, 0))

    def partner(step):
        bit, total = 1, 0
        while bit < n_off:
            total = total + bit * lax.rem(lax.rem(lax.div(o, bit), 2) + lax.rem(lax.div(step, bit), 2), 2)
            bit *= 2
        return total

    def xy_copy(step):
        p = partner(jnp.int32(step))
        return pltpu.make_async_remote_copy(
            src_ref=send.at[p], dst_ref=buf.at[i, o], send_sem=xy_sem.at[step], recv_sem=recv_sem.at[i, o],
            device_id=(p, i), device_id_type=MESH)

    def chunk_copy(j, q, sems, target):
        return pltpu.make_async_remote_copy(
            src_ref=buf.at[j, q], dst_ref=buf.at[j, q], send_sem=sems.at[j, q], recv_sem=recv_sem.at[j, q],
            device_id=(o, target), device_id_type=MESH)

    def arrived(j, q):
        pltpu.make_async_remote_copy(
            src_ref=buf.at[j, q], dst_ref=buf.at[j, q], send_sem=sib_sem.at[j, q], recv_sem=recv_sem.at[j, q],
            device_id=(o, sibling), device_id_type=MESH).wait_recv()

    for step in range(1, n_off):
        xy_copy(step).start()

    def out_copy(j, q):
        return pltpu.make_async_copy(levels.at[:, j, q], out.at[:, j, q], out_sem.at[j, q])

    def filter_chunk(j, q):
        samples = buf.shape[3]
        width = samples + 128
        gap = jnp.zeros((per, 128), jnp.float32)
        values = jnp.concatenate([buf[j, q].astype(jnp.float32), gap], axis=1)
        boosted = values - 0.5 * (pltpu.roll(values, 1, 1) + pltpu.roll(values, width - 1, 1))
        boosted = boosted[:, :samples]
        wide = jnp.concatenate([boosted, gap], axis=1)
        smoothed = (
            3.0 * wide
            + 2.0 * (pltpu.roll(wide, 1, 1) + pltpu.roll(wide, width - 1, 1))
            + pltpu.roll(wide, 2, 1)
            + pltpu.roll(wide, width - 2, 1)
        ) / 9.0
        levels[0, j, q] = boosted.astype(jnp.bfloat16)
        levels[1, j, q] = smoothed[:, :samples].astype(jnp.bfloat16)
        out_copy(j, q).start()

    def first_chunk(step, carry):
        q = partner(step)

        @pl.when(step > 0)
        def _():
            arrived(i, q)

        @pl.when(has_up)
        def _():
            chunk_copy(i, q, up_sem, i + 2).start()

        @pl.when(has_down)
        def _():
            chunk_copy(i, q, down_sem, i - 2).start()

        chunk_copy(i, q, sib_sem, sibling).start()
        filter_chunk(i, q)
        return carry

    lax.fori_loop(0, n_off, first_chunk, 0)

    def one_chunk(turn, carry):
        d = lax.div(turn, n_off) + 1
        q = partner(lax.rem(turn, n_off))
        below = i - 2 * d
        above = i + 2 * d
        from_below = z >= d
        from_above = z + d < lines

        @pl.when(from_below)
        def _():
            arrived(below, q)

            @pl.when(has_up)
            def _():
                chunk_copy(below, q, up_sem, i + 2).start()

            chunk_copy(below, q, sib_sem, sibling).start()

        @pl.when(from_above)
        def _():
            arrived(above, q)

            @pl.when(has_down)
            def _():
                chunk_copy(above, q, down_sem, i - 2).start()

            chunk_copy(above, q, sib_sem, sibling).start()

        @pl.when(from_below)
        def _():
            filter_chunk(below, q)

        @pl.when(from_above)
        def _():
            filter_chunk(above, q)

        near = d - 1

        @pl.when(z >= near)
        def _():
            arrived(sibling - 2 * near, q)
            filter_chunk(sibling - 2 * near, q)

        @pl.when(jnp.logical_and(near > 0, z + near < lines))
        def _():
            arrived(sibling + 2 * near, q)
            filter_chunk(sibling + 2 * near, q)

        return carry

    lax.fori_loop(0, lines * n_off, one_chunk, 0)

    for w in range(lines):

        def last(q, carry):
            mine = 2 * w + core
            out_copy(2 * w, q).wait()
            out_copy(2 * w + 1, q).wait()
            chunk_copy(mine, q, sib_sem, sibling).wait_send()

            @pl.when(jnp.logical_and(has_up, w <= z))
            def _():
                chunk_copy(mine, q, up_sem, i + 2).wait_send()

            @pl.when(jnp.logical_and(has_down, w >= z))
            def _():
                chunk_copy(mine, q, down_sem, i - 2).wait_send()

            return carry

        lax.fori_loop(0, n_off, last, 0)

    for step in range(1, n_off):
        xy_copy(step).wait_send()


def gather_levels(traces, offset_bins, class_slots):
    n_off = lax.axis_size("off")
    n_img = lax.axis_size("img")
    rows, samples = traces.shape
    per = rows // n_off
    hbm = pl.BlockSpec(memory_space=pl.ANY)
    return pl.pallas_call(
        functools.partial(gather_kernel, n_off, n_img),
        out_shape=jax.ShapeDtypeStruct((2, n_img, n_off, per, samples), jnp.bfloat16),
        in_specs=[hbm] * 3,
        out_specs=hbm,
        scratch_shapes=[
            pltpu.VMEM((rows, samples), jnp.bfloat16),
            pltpu.VMEM((1, rows), jnp.int32),
            pltpu.VMEM((1, rows), jnp.int32),
            pltpu.VMEM((n_img, n_off, per, samples), jnp.bfloat16),
            pltpu.VMEM((2, n_img, n_off, per, samples), jnp.bfloat16),
            pltpu.VMEM((n_off, per, samples), jnp.bfloat16),
            pltpu.SemaphoreType.DMA((3,)),
            pltpu.SemaphoreType.DMA((n_off,)),
            pltpu.SemaphoreType.DMA((n_img, n_off)),
            pltpu.SemaphoreType.DMA((n_img, n_off)),
            pltpu.SemaphoreType.DMA((n_img, n_off)),
            pltpu.SemaphoreType.DMA((n_img, n_off)),
            pltpu.SemaphoreType.DMA((n_img, n_off)),
        ],
        compiler_params=pltpu.CompilerParams(
            collective_id=0, has_side_effects=True, vmem_limit_bytes=56 * 1024 * 1024),
        name="gather_levels",
    )(traces, offset_bins.reshape(1, rows), class_slots.reshape(1, rows))


def migrate_kernel(band_ref, smooth_ref, levels, weights_ref, out_ref, segments, sems):
    samples = levels.shape[2]
    span = segments.shape[2]
    blocks = segments.shape[0]
    block = pl.program_id(0)

    def base_of(b):
        return jnp.minimum(lax.div(band_ref[b], 128), (samples - span) // 128) * 128

    def segment_copy(b):
        band = pl.ds(pl.multiple_of(base_of(b), 128), span)
        return pltpu.make_async_copy(levels.at[smooth_ref[b], :, band], segments.at[b], sems.at[b])

    @pl.when(block == 0)
    def _():
        for b in range(blocks):
            segment_copy(b).start()

    segment_copy(block).wait()
    shift = band_ref[block] - base_of(block)
    product = jnp.dot(weights_ref[...], segments[block], preferred_element_type=jnp.float32)
    turned = pltpu.roll(product, lax.rem(span - shift, span), 1)
    out_ref[...] = turned[:, :NT].astype(jnp.bfloat16)


def migrate(levels, weight_rows, band_rows, smooth_rows):
    rows = levels.shape[1]
    columns = weight_rows.shape[0]
    blocks = columns // CB
    return pl.pallas_call(
        migrate_kernel,
        out_shape=jax.ShapeDtypeStruct((columns, NT), jnp.bfloat16),
        grid_spec=pltpu.PrefetchScalarGridSpec(
            num_scalar_prefetch=2,
            grid=(blocks,),
            in_specs=[
                pl.BlockSpec(memory_space=pltpu.HBM),
                pl.BlockSpec((CB, rows), lambda b, *_: (b, 0)),
            ],
            out_specs=pl.BlockSpec((CB, NT), lambda b, *_: (b, 0)),
            scratch_shapes=[
                pltpu.VMEM((blocks, rows, NT + 128), jnp.bfloat16),
                pltpu.SemaphoreType.DMA((blocks,)),
            ],
        ),
        compiler_params=pltpu.CompilerParams(vmem_limit_bytes=62 * 1024 * 1024),
        name="migrate",
    )(band_rows, smooth_rows, levels, weight_rows)


def per_device(traces, offset_bins, class_slots, weights, band_start, smoothing):
    levels = gather_levels(traces, offset_bins, class_slots)
    levels = levels.reshape(2, -1, traces.shape[1])
    return migrate(levels, weights[0], band_start[0], smoothing[0])[None]


def solution(mesh):
    in_specs = (
        P(("off", "img"), None),
        P(("off", "img")),
        P(("off", "img")),
        P("off", "img", None),
        P("off", "img"),
        P("off", "img"),
    )
    out_specs = P("off", "img", None)
    return jax.shard_map(
        per_device, mesh=mesh, in_specs=in_specs, out_specs=out_specs, check_vma=False
    )
```

```python
import functools

import jax
import jax.numpy as jnp
from jax import lax
from jax.experimental import pallas as pl
from jax.experimental.pallas import tpu as pltpu
from jax.sharding import PartitionSpec as P

NT = 1536
CB = 128
MESH = pl.DeviceIdType.MESH


def gather_kernel(n_off, n_img, traces_hbm, bins_hbm, slots_hbm, out, traces_ref, bins_ref, slots_ref, buf, levels, send,
                  in_sem, xy_sem, up_sem, down_sem, sib_sem, recv_sem, out_sem):
    o = lax.axis_index("off")
    i = lax.axis_index("img")
    rows = traces_ref.shape[0]
    per = rows // n_off
    lines = n_img // 2
    z = i // 2
    core = i % 2
    sibling = z * 2 + 1 - core
    has_up = z < lines - 1
    has_down = z > 0

    inputs = [
        pltpu.make_async_copy(source, held, in_sem.at[n])
        for n, (source, held) in enumerate(
            [(traces_hbm, traces_ref), (bins_hbm, bins_ref), (slots_hbm, slots_ref)])
    ]
    for copy in inputs:
        copy.start()

    barrier = pltpu.get_barrier_semaphore()
    for step in range(1, n_off):
        pl.semaphore_signal(barrier, inc=1, device_id=((o + step) % n_off, i), device_id_type=MESH)
    pl.semaphore_signal(barrier, inc=1, device_id=(o, sibling), device_id_type=MESH)

    @pl.when(has_up)
    def _():
        pl.semaphore_signal(barrier, inc=1, device_id=(o, i + 2), device_id_type=MESH)

    @pl.when(has_down)
    def _():
        pl.semaphore_signal(barrier, inc=1, device_id=(o, i - 2), device_id_type=MESH)

    for copy in inputs:
        copy.wait()
    targets = bins_ref[...] * per + slots_ref[...]
    onehot = jnp.where(lax.broadcasted_iota(jnp.int32, (rows, rows), 0) == targets, 1.0, 0.0).astype(jnp.bfloat16)
    ordered = jnp.dot(onehot, traces_ref[...], preferred_element_type=jnp.float32)
    for p in range(n_off):
        send[p] = ordered[p * per:(p + 1) * per].astype(jnp.bfloat16)
    buf[i, o] = send[o]

    pl.semaphore_wait(barrier, n_off + jnp.where(has_up, 1, 0) + jnp.where(has_down, 1, 0))

    def partner(step):
        bit, total = 1, 0
        while bit < n_off:
            total = total + bit * lax.rem(lax.rem(lax.div(o, bit), 2) + lax.rem(lax.div(step, bit), 2), 2)
            bit *= 2
        return total

    def xy_copy(step):
        p = partner(jnp.int32(step))
        return pltpu.make_async_remote_copy(
            src_ref=send.at[p], dst_ref=buf.at[i, o], send_sem=xy_sem.at[step], recv_sem=recv_sem.at[i, o],
            device_id=(p, i), device_id_type=MESH)

    def chunk_copy(j, q, sems, target):
        return pltpu.make_async_remote_copy(
            src_ref=buf.at[j, q], dst_ref=buf.at[j, q], send_sem=sems.at[j, q], recv_sem=recv_sem.at[j, q],
            device_id=(o, target), device_id_type=MESH)

    def arrived(j, q):
        pltpu.make_async_remote_copy(
            src_ref=buf.at[j, q], dst_ref=buf.at[j, q], send_sem=sib_sem.at[j, q], recv_sem=recv_sem.at[j, q],
            device_id=(o, sibling), device_id_type=MESH).wait_recv()

    for step in range(1, n_off):
        xy_copy(step).start()

    def out_copy(j, q):
        return pltpu.make_async_copy(levels.at[:, j, q], out.at[:, j, q], out_sem.at[j, q])

    def filter_chunk(j, q):
        samples = buf.shape[3]
        width = samples + 128
        gap = jnp.zeros((per, 128), jnp.float32)
        values = jnp.concatenate([buf[j, q].astype(jnp.float32), gap], axis=1)
        boosted = values - 0.5 * (pltpu.roll(values, 1, 1) + pltpu.roll(values, width - 1, 1))
        boosted = boosted[:, :samples]
        wide = jnp.concatenate([boosted, gap], axis=1)
        smoothed = (
            3.0 * wide
            + 2.0 * (pltpu.roll(wide, 1, 1) + pltpu.roll(wide, width - 1, 1))
            + pltpu.roll(wide, 2, 1)
            + pltpu.roll(wide, width - 2, 1)
        ) / 9.0
        levels[0, j, q] = boosted.astype(jnp.bfloat16)
        levels[1, j, q] = smoothed[:, :samples].astype(jnp.bfloat16)
        out_copy(j, q).start()

    def first_chunk(step, carry):
        q = partner(step)

        @pl.when(step > 0)
        def _():
            arrived(i, q)

        @pl.when(has_up)
        def _():
            chunk_copy(i, q, up_sem, i + 2).start()

        @pl.when(has_down)
        def _():
            chunk_copy(i, q, down_sem, i - 2).start()

        chunk_copy(i, q, sib_sem, sibling).start()
        filter_chunk(i, q)
        return carry

    lax.fori_loop(0, n_off, first_chunk, 0)

    def one_chunk(turn, carry):
        d = lax.div(turn, n_off) + 1
        q = partner(lax.rem(turn, n_off))
        below = i - 2 * d
        above = i + 2 * d
        from_below = z >= d
        from_above = z + d < lines

        @pl.when(from_below)
        def _():
            arrived(below, q)

            @pl.when(has_up)
            def _():
                chunk_copy(below, q, up_sem, i + 2).start()

            chunk_copy(below, q, sib_sem, sibling).start()

        @pl.when(from_above)
        def _():
            arrived(above, q)

            @pl.when(has_down)
            def _():
                chunk_copy(above, q, down_sem, i - 2).start()

            chunk_copy(above, q, sib_sem, sibling).start()

        @pl.when(from_below)
        def _():
            filter_chunk(below, q)

        @pl.when(from_above)
        def _():
            filter_chunk(above, q)

        near = d - 1

        @pl.when(z >= near)
        def _():
            arrived(sibling - 2 * near, q)
            filter_chunk(sibling - 2 * near, q)

        @pl.when(jnp.logical_and(near > 0, z + near < lines))
        def _():
            arrived(sibling + 2 * near, q)
            filter_chunk(sibling + 2 * near, q)

        return carry

    lax.fori_loop(0, lines * n_off, one_chunk, 0)

    for w in range(lines):

        def last(q, carry):
            mine = 2 * w + core
            out_copy(2 * w, q).wait()
            out_copy(2 * w + 1, q).wait()
            chunk_copy(mine, q, sib_sem, sibling).wait_send()

            @pl.when(jnp.logical_and(has_up, w <= z))
            def _():
                chunk_copy(mine, q, up_sem, i + 2).wait_send()

            @pl.when(jnp.logical_and(has_down, w >= z))
            def _():
                chunk_copy(mine, q, down_sem, i - 2).wait_send()

            return carry

        lax.fori_loop(0, n_off, last, 0)

    for step in range(1, n_off):
        xy_copy(step).wait_send()


def gather_levels(traces, offset_bins, class_slots):
    n_off = lax.axis_size("off")
    n_img = lax.axis_size("img")
    rows, samples = traces.shape
    per = rows // n_off
    hbm = pl.BlockSpec(memory_space=pl.ANY)
    return pl.pallas_call(
        functools.partial(gather_kernel, n_off, n_img),
        out_shape=pltpu.VMEM((2, n_img, n_off, per, samples), jnp.bfloat16),
        in_specs=[hbm] * 3,
        out_specs=hbm,
        scratch_shapes=[
            pltpu.VMEM((rows, samples), jnp.bfloat16),
            pltpu.VMEM((1, rows), jnp.int32),
            pltpu.VMEM((1, rows), jnp.int32),
            pltpu.VMEM((n_img, n_off, per, samples), jnp.bfloat16),
            pltpu.VMEM((2, n_img, n_off, per, samples), jnp.bfloat16),
            pltpu.VMEM((n_off, per, samples), jnp.bfloat16),
            pltpu.SemaphoreType.DMA((3,)),
            pltpu.SemaphoreType.DMA((n_off,)),
            pltpu.SemaphoreType.DMA((n_img, n_off)),
            pltpu.SemaphoreType.DMA((n_img, n_off)),
            pltpu.SemaphoreType.DMA((n_img, n_off)),
            pltpu.SemaphoreType.DMA((n_img, n_off)),
            pltpu.SemaphoreType.DMA((n_img, n_off)),
        ],
        compiler_params=pltpu.CompilerParams(
            collective_id=0, has_side_effects=True,
            vmem_limit_bytes=60 * 1024 * 1024 - 4 * n_img * rows * samples),
        name="gather_levels",
    )(traces, offset_bins.reshape(1, rows), class_slots.reshape(1, rows))


def migrate_kernel(band_ref, smooth_ref, levels, weights_ref, out_ref):
    samples = levels.shape[2]
    span = NT + 128
    block = pl.program_id(0)
    base = jnp.minimum(lax.div(band_ref[block], 128), (samples - span) // 128) * 128
    shift = band_ref[block] - base
    segment = levels[smooth_ref[block], :, pl.ds(pl.multiple_of(base, 128), span)]
    product = jnp.dot(weights_ref[...], segment, preferred_element_type=jnp.float32)
    turned = pltpu.roll(product, lax.rem(span - shift, span), 1)
    out_ref[...] = turned[:, :NT].astype(jnp.bfloat16)


def migrate(levels, weight_rows, band_rows, smooth_rows):
    rows = levels.shape[1]
    columns = weight_rows.shape[0]
    return pl.pallas_call(
        migrate_kernel,
        out_shape=jax.ShapeDtypeStruct((columns, NT), jnp.bfloat16),
        grid_spec=pltpu.PrefetchScalarGridSpec(
            num_scalar_prefetch=2,
            grid=(columns // CB,),
            in_specs=[
                pl.BlockSpec(memory_space=pltpu.VMEM),
                pl.BlockSpec((CB, rows), lambda b, *_: (b, 0)),
            ],
            out_specs=pl.BlockSpec((CB, NT), lambda b, *_: (b, 0)),
        ),
        compiler_params=pltpu.CompilerParams(vmem_limit_bytes=40 * 1024 * 1024),
        name="migrate",
    )(band_rows, smooth_rows, levels, weight_rows)


def per_device(traces, offset_bins, class_slots, weights, band_start, smoothing):
    levels = gather_levels(traces, offset_bins, class_slots)
    levels = levels.reshape(2, -1, traces.shape[1])
    return migrate(levels, weights[0], band_start[0], smoothing[0])[None]


def solution(mesh):
    in_specs = (
        P(("off", "img"), None),
        P(("off", "img")),
        P(("off", "img")),
        P("off", "img", None),
        P("off", "img"),
        P("off", "img"),
    )
    out_specs = P("off", "img", None)
    return jax.shard_map(
        per_device, mesh=mesh, in_specs=in_specs, out_specs=out_specs, check_vma=False
    )
```

```python
import functools

import jax
import jax.numpy as jnp
from jax import lax
from jax.experimental import pallas as pl
from jax.experimental.pallas import tpu as pltpu
from jax.sharding import PartitionSpec as P

NT = 1536
CB = 128
MESH = pl.DeviceIdType.MESH


def gather_kernel(n_off, n_img, traces_hbm, bins_hbm, slots_hbm, levels, traces_ref, bins_ref, slots_ref, buf, send,
                  in_sem, xy_sem, up_sem, down_sem, sib_sem, recv_sem):
    o = lax.axis_index("off")
    i = lax.axis_index("img")
    rows = traces_ref.shape[0]
    per = rows // n_off
    lines = n_img // 2
    z = i // 2
    core = i % 2
    sibling = z * 2 + 1 - core
    has_up = z < lines - 1
    has_down = z > 0

    inputs = [
        pltpu.make_async_copy(source, held, in_sem.at[n])
        for n, (source, held) in enumerate(
            [(traces_hbm, traces_ref), (bins_hbm, bins_ref), (slots_hbm, slots_ref)])
    ]
    for copy in inputs:
        copy.start()

    barrier = pltpu.get_barrier_semaphore()
    for step in range(1, n_off):
        pl.semaphore_signal(barrier, inc=1, device_id=((o + step) % n_off, i), device_id_type=MESH)
    pl.semaphore_signal(barrier, inc=1, device_id=(o, sibling), device_id_type=MESH)

    @pl.when(has_up)
    def _():
        pl.semaphore_signal(barrier, inc=1, device_id=(o, i + 2), device_id_type=MESH)

    @pl.when(has_down)
    def _():
        pl.semaphore_signal(barrier, inc=1, device_id=(o, i - 2), device_id_type=MESH)

    for copy in inputs:
        copy.wait()
    targets = bins_ref[...] * per + slots_ref[...]
    onehot = jnp.where(lax.broadcasted_iota(jnp.int32, (rows, rows), 0) == targets, 1.0, 0.0).astype(jnp.bfloat16)
    ordered = jnp.dot(onehot, traces_ref[...], preferred_element_type=jnp.float32)
    for p in range(n_off):
        send[p] = ordered[p * per:(p + 1) * per].astype(jnp.bfloat16)
    buf[i, o] = send[o]

    pl.semaphore_wait(barrier, n_off + jnp.where(has_up, 1, 0) + jnp.where(has_down, 1, 0))

    def partner(step):
        bit, total = 1, 0
        while bit < n_off:
            total = total + bit * lax.rem(lax.rem(lax.div(o, bit), 2) + lax.rem(lax.div(step, bit), 2), 2)
            bit *= 2
        return total

    def xy_copy(step):
        p = partner(jnp.int32(step))
        return pltpu.make_async_remote_copy(
            src_ref=send.at[p], dst_ref=buf.at[i, o], send_sem=xy_sem.at[step], recv_sem=recv_sem.at[i, o],
            device_id=(p, i), device_id_type=MESH)

    def chunk_copy(j, q, sems, target):
        return pltpu.make_async_remote_copy(
            src_ref=buf.at[j, q], dst_ref=buf.at[j, q], send_sem=sems.at[j, q], recv_sem=recv_sem.at[j, q],
            device_id=(o, target), device_id_type=MESH)

    def arrived(j, q):
        pltpu.make_async_remote_copy(
            src_ref=buf.at[j, q], dst_ref=buf.at[j, q], send_sem=sib_sem.at[j, q], recv_sem=recv_sem.at[j, q],
            device_id=(o, sibling), device_id_type=MESH).wait_recv()

    for step in range(1, n_off):
        xy_copy(step).start()

    def filter_chunk(j, q):
        samples = buf.shape[3]
        width = samples + 128
        gap = jnp.zeros((per, 128), jnp.float32)
        values = jnp.concatenate([buf[j, q].astype(jnp.float32), gap], axis=1)
        boosted = values - 0.5 * (pltpu.roll(values, 1, 1) + pltpu.roll(values, width - 1, 1))
        boosted = boosted[:, :samples]
        wide = jnp.concatenate([boosted, gap], axis=1)
        smoothed = (
            3.0 * wide
            + 2.0 * (pltpu.roll(wide, 1, 1) + pltpu.roll(wide, width - 1, 1))
            + pltpu.roll(wide, 2, 1)
            + pltpu.roll(wide, width - 2, 1)
        ) / 9.0
        levels[0, j, q] = boosted.astype(jnp.bfloat16)
        levels[1, j, q] = smoothed[:, :samples].astype(jnp.bfloat16)

    def first_chunk(step, carry):
        q = partner(step)

        @pl.when(step > 0)
        def _():
            arrived(i, q)

        @pl.when(has_up)
        def _():
            chunk_copy(i, q, up_sem, i + 2).start()

        @pl.when(has_down)
        def _():
            chunk_copy(i, q, down_sem, i - 2).start()

        chunk_copy(i, q, sib_sem, sibling).start()
        filter_chunk(i, q)
        return carry

    lax.fori_loop(0, n_off, first_chunk, 0)

    def one_chunk(turn, carry):
        d = lax.div(turn, n_off) + 1
        q = partner(lax.rem(turn, n_off))
        below = i - 2 * d
        above = i + 2 * d
        from_below = z >= d
        from_above = z + d < lines

        @pl.when(from_below)
        def _():
            arrived(below, q)

            @pl.when(has_up)
            def _():
                chunk_copy(below, q, up_sem, i + 2).start()

            chunk_copy(below, q, sib_sem, sibling).start()

        @pl.when(from_above)
        def _():
            arrived(above, q)

            @pl.when(has_down)
            def _():
                chunk_copy(above, q, down_sem, i - 2).start()

            chunk_copy(above, q, sib_sem, sibling).start()

        @pl.when(from_below)
        def _():
            filter_chunk(below, q)

        @pl.when(from_above)
        def _():
            filter_chunk(above, q)

        near = d - 1

        @pl.when(z >= near)
        def _():
            arrived(sibling - 2 * near, q)
            filter_chunk(sibling - 2 * near, q)

        @pl.when(jnp.logical_and(near > 0, z + near < lines))
        def _():
            arrived(sibling + 2 * near, q)
            filter_chunk(sibling + 2 * near, q)

        return carry

    lax.fori_loop(0, lines * n_off, one_chunk, 0)

    for w in range(lines):

        def last(q, carry):
            mine = 2 * w + core
            chunk_copy(mine, q, sib_sem, sibling).wait_send()

            @pl.when(jnp.logical_and(has_up, w <= z))
            def _():
                chunk_copy(mine, q, up_sem, i + 2).wait_send()

            @pl.when(jnp.logical_and(has_down, w >= z))
            def _():
                chunk_copy(mine, q, down_sem, i - 2).wait_send()

            return carry

        lax.fori_loop(0, n_off, last, 0)

    for step in range(1, n_off):
        xy_copy(step).wait_send()


def gather_levels(traces, offset_bins, class_slots):
    n_off = lax.axis_size("off")
    n_img = lax.axis_size("img")
    rows, samples = traces.shape
    per = rows // n_off
    hbm = pl.BlockSpec(memory_space=pl.ANY)
    return pl.pallas_call(
        functools.partial(gather_kernel, n_off, n_img),
        out_shape=pltpu.VMEM((2, n_img, n_off, per, samples), jnp.bfloat16),
        in_specs=[hbm] * 3,
        out_specs=pl.BlockSpec(memory_space=pltpu.VMEM),
        scratch_shapes=[
            pltpu.VMEM((rows, samples), jnp.bfloat16),
            pltpu.VMEM((1, rows), jnp.int32),
            pltpu.VMEM((1, rows), jnp.int32),
            pltpu.VMEM((n_img, n_off, per, samples), jnp.bfloat16),
            pltpu.VMEM((n_off, per, samples), jnp.bfloat16),
            pltpu.SemaphoreType.DMA((3,)),
            pltpu.SemaphoreType.DMA((n_off,)),
            pltpu.SemaphoreType.DMA((n_img, n_off)),
            pltpu.SemaphoreType.DMA((n_img, n_off)),
            pltpu.SemaphoreType.DMA((n_img, n_off)),
            pltpu.SemaphoreType.DMA((n_img, n_off)),
        ],
        compiler_params=pltpu.CompilerParams(
            collective_id=0, has_side_effects=True,
            vmem_limit_bytes=60 * 1024 * 1024 - 4 * n_img * rows * samples),
        name="gather_levels",
    )(traces, offset_bins.reshape(1, rows), class_slots.reshape(1, rows))


def migrate_kernel(band_ref, smooth_ref, levels, weights_ref, out_ref):
    samples = levels.shape[2]
    span = NT + 128
    block = pl.program_id(0)
    base = jnp.minimum(lax.div(band_ref[block], 128), (samples - span) // 128) * 128
    shift = band_ref[block] - base
    segment = levels[smooth_ref[block], :, pl.ds(pl.multiple_of(base, 128), span)]
    product = jnp.dot(weights_ref[...], segment, preferred_element_type=jnp.float32)
    turned = pltpu.roll(product, lax.rem(span - shift, span), 1)
    out_ref[...] = turned[:, :NT].astype(jnp.bfloat16)


def migrate(levels, weight_rows, band_rows, smooth_rows):
    rows = levels.shape[1]
    columns = weight_rows.shape[0]
    return pl.pallas_call(
        migrate_kernel,
        out_shape=jax.ShapeDtypeStruct((columns, NT), jnp.bfloat16),
        grid_spec=pltpu.PrefetchScalarGridSpec(
            num_scalar_prefetch=2,
            grid=(columns // CB,),
            in_specs=[
                pl.BlockSpec(memory_space=pltpu.VMEM),
                pl.BlockSpec((CB, rows), lambda b, *_: (b, 0)),
            ],
            out_specs=pl.BlockSpec((CB, NT), lambda b, *_: (b, 0)),
        ),
        compiler_params=pltpu.CompilerParams(vmem_limit_bytes=40 * 1024 * 1024),
        name="migrate",
    )(band_rows, smooth_rows, levels, weight_rows)


def per_device(traces, offset_bins, class_slots, weights, band_start, smoothing):
    levels = gather_levels(traces, offset_bins, class_slots)
    levels = levels.reshape(2, -1, traces.shape[1])
    return migrate(levels, weights[0], band_start[0], smoothing[0])[None]


def solution(mesh):
    in_specs = (
        P(("off", "img"), None),
        P(("off", "img")),
        P(("off", "img")),
        P("off", "img", None),
        P("off", "img"),
        P("off", "img"),
    )
    out_specs = P("off", "img", None)
    return jax.shard_map(
        per_device, mesh=mesh, in_specs=in_specs, out_specs=out_specs, check_vma=False
    )
```
